32 devices in a mesh: basin: 8 (over z, x), event: 4 (over y, core).
Axes of the slice: x: 2, y: 2, z: 4, core: 2. Of those that a mesh axis runs over, the one named last changes fastest.
Arguments:
- reach_attrs: bfloat16 [12288, 32], P('basin'), may hold values from -6 to 6
- w_first: bfloat16 [32, 768], replicated, may hold values from -1 to 1
- b_first: float32 [768], replicated, may hold values from -3 to 3
- w_second: bfloat16 [768, 768], replicated, may hold values from -0.21875 to 0.21875
- b_second: float32 [768], replicated, may hold values from -3 to 3
- w_out: bfloat16 [768], replicated, may hold values from -0.21875 to 0.21875
- section_factor: float32 [10], replicated, may hold values from 0.5 to 2
- bed_slope: float32 [12288], P('basin'), may hold values from 0.0001 to 0.004
- seg_count: int32 [12288], P('basin'), may hold values from 1 to 8
- section_class: int32 [12288], P('basin'), may hold values from 0 to 9
- down_local: int32 [12288], P('basin'), may hold values from 0 to 1536, as said below
- send_list: int32 [8, 8, 24], P('basin'), may hold values from 0 to 1536, as said below
- recv_list: int32 [8, 8, 24], P('basin'), may hold values from 0 to 1536, as said below
- area_start: float32 [128, 12288], P('event', 'basin'), may hold values from 0.2 to 2
- lateral: float32 [3, 128, 12288], P(None, 'event', 'basin'), may hold values from 0.05 to 1
- cotangent: float32 [128, 12288], P('event', 'basin'), may hold values from -6 to 6
Outputs:
- outflow: float32 [128, 12288], P('event', 'basin')
- grad_lateral: float32 [3, 128, 12288], P(None, 'event', 'basin')
- grad_w_first: float32 [32, 768], replicated
- grad_b_first: float32 [768], replicated
- grad_w_second: float32 [768, 768], replicated
- grad_b_second: float32 [768], replicated
- grad_w_out: float32 [768], replicated
The draws below stay inside these ranges and needn't reach their ends.
Inputs may be any that keep to these rules, and one draw needn't show every extreme that they name: `down_local`: the downstream reach of a reach in its own sub-basin, as a local index 1 to 8 above the reach's own; 1536 where the reach drains into another sub-basin (it is then listed in send_list) or leaves the network. send_list[s, d, c] is a local reach of sub-basin s whose end flow enters sub-basin d, or 1536 for an empty slot; live slots come first in each list and no reach is listed twice. Only the lists from s to (s + 1), (s + 2), (s + 4) and (s + 7) mod 8 can hold live slots; those to (s + 1), (s + 4) and (s + 7) are always full, the one to (s + 2) is empty or holds 12 or more. One sub-basin receives 24 from each of the four sub-basins that can drain into it. recv_list[d, s, c] is the local reach of sub-basin d that receives slot c of send_list[s, d], and is 1536 exactly where that slot is empty; no reach is a target twice.
All inputs are finite; a program needn't handle non-finite values.
Results may differ from the reference program's by a relative error of at most 0.02.
Values sent between devices are 32-bit elements; how exact they have to be, the bound alone decides.
A program may use at most 64 MiB of HBM per device.

```python
import math
import jax
import jax.numpy as jnp
from jax import lax

FEAT = 32
HID = 768
NCLASS = 10
SEGMAX = 8
STEPS = 3
CAP = 24
R_DEV = 1536
REACHES = 12288
EVENTS = 128


def topology(key):
    basins = REACHES // R_DEV
    base_key = jax.random.fold_in(key, 11)
    key_two = jax.random.fold_in(base_key, 0)
    key_on = jax.random.fold_in(base_key, 2)
    key_busy = jax.random.fold_in(base_key, 3)
    key_send = jax.random.fold_in(base_key, 4)
    key_recv = jax.random.fold_in(base_key, 5)
    key_down = jax.random.fold_in(base_key, 6)
    row_index = jnp.arange(basins, dtype=jnp.int32)[:, None]
    col_index = jnp.arange(basins, dtype=jnp.int32)[None, :]
    offset = (col_index - row_index) % basins
    count_two = jax.random.randint(key_two, (basins, basins), CAP // 2, CAP + 1)
    switch_on = jax.random.randint(key_on, (basins, basins), 0, 2)
    count_two = jnp.where(switch_on == 1, count_two, 0)
    always_full = (offset == 1) | (offset == basins // 2) | (offset == basins - 1)
    slot_count = jnp.where(always_full, CAP, jnp.where(offset == 2, count_two, 0))
    busiest = jax.random.randint(key_busy, (), 0, basins)
    full_pair = (col_index == busiest) & (offset == 2)
    slot_count = jnp.where(full_pair, CAP, slot_count)
    live_slot = jnp.arange(CAP, dtype=jnp.int32)[None, None, :] < slot_count[:, :, None]
    send_order = jax.vmap(lambda one_key: jax.random.permutation(one_key, R_DEV))(jax.random.split(key_send, basins))
    send_pick = send_order[:, :basins * CAP].reshape(basins, basins, CAP)
    send_list = jnp.where(live_slot, send_pick, R_DEV).astype(jnp.int32)
    recv_order = jax.vmap(lambda one_key: jax.random.permutation(one_key, R_DEV))(jax.random.split(key_recv, basins))
    recv_pick = recv_order[:, :basins * CAP].reshape(basins, basins, CAP)
    recv_list = jnp.where(jnp.transpose(live_slot, (1, 0, 2)), recv_pick, R_DEV).astype(jnp.int32)
    hop_sizes = jax.random.randint(key_down, (basins, R_DEV), 1, 9)
    next_reach = jnp.arange(R_DEV, dtype=jnp.int32)[None, :] + hop_sizes
    next_reach = jnp.where(next_reach >= R_DEV, R_DEV, next_reach)
    sender_mark = jnp.zeros((basins, R_DEV + 1), jnp.int32).at[row_index, send_list.reshape(basins, basins * CAP)].set(1)
    down_local = jnp.where(sender_mark[:, :R_DEV] == 1, R_DEV, next_reach).reshape(REACHES).astype(jnp.int32)
    return (down_local, send_list, recv_list)


def draw_down_local(key, part):
    return topology(key)[0]


def draw_send_list(key, part):
    return topology(key)[1]


def draw_recv_list(key, part):
    return topology(key)[2]


def set_ends(result, own_key, low, top_value):
    longest = result.shape.index(max(result.shape))
    spots = []
    for shift in (0, 1):
        where = [jax.random.randint(jax.random.fold_in(own_key, axis), (), 0, length) for axis, length in enumerate(result.shape)]
        where[longest] = (where[longest] + shift) % result.shape[longest]
        spots.append(tuple(where))
    return result.at[spots[0]].set(low).at[spots[1]].set(top_value)


def levels(own_key, extent, shards, low, largest):
    loudness, own = 1.0, jax.random.fold_in(own_key, 6)
    for position, shards_of in shards:
        heights = jnp.exp(jax.random.uniform(jax.random.fold_in(own, position), (shards_of,), jnp.float32, low / len(shards), largest / len(shards)))
        loudness = loudness * jnp.repeat(heights, extent[position] // shards_of).reshape([-1 if axis == position else 1 for axis in range(len(extent))])
    return loudness


def bell_draw(own_key, extent, scale, most, cuts=(), held_as=jnp.bfloat16):
    drawn = scale * jax.random.normal(own_key, extent, jnp.float32)
    if cuts:
        drawn = drawn * levels(own_key, extent, cuts, -0.22, 0.18)
    return jnp.clip(drawn, -most, most).astype(held_as)


def setup_inputs(seed: int = 0) -> dict:
    keys = jax.random.split(jax.random.key(seed), 17)
    return {
        "reach_attrs": bell_draw(keys[0], (REACHES, FEAT), 1.0, 6.0, ((0, 8),)),
        "w_first": bell_draw(keys[1], (FEAT, HID), FEAT ** -0.5, 1.0),
        "b_first": bell_draw(keys[2], (HID,), 0.5, 3.0, (), jnp.float32),
        "w_second": bell_draw(keys[3], (HID, HID), HID ** -0.5, 0.21875),
        "b_second": bell_draw(keys[4], (HID,), 0.5, 3.0, (), jnp.float32),
        "w_out": bell_draw(keys[5], (HID,), HID ** -0.5, 0.21875),
        "section_factor": jnp.clip(jnp.exp(jax.random.uniform(keys[6], (NCLASS,), jnp.float32, math.log(0.5), math.log(2.0))), 0.5, 2.0),
        "bed_slope": jnp.clip(jnp.exp(math.log(0.004) - 3.6888795 * jax.random.uniform(keys[7], (REACHES,), jnp.float32) ** levels(keys[7], (REACHES,), ((0, 8),), -0.2, 0.2)), 0.0001, 0.004),
        "seg_count": set_ends(jax.random.randint(keys[8], (REACHES,), 1, SEGMAX + 1), jax.random.fold_in(keys[8], 1), 1, SEGMAX).astype(jnp.int32),
        "section_class": set_ends(jax.random.randint(keys[9], (REACHES,), 0, NCLASS), jax.random.fold_in(keys[9], 1), 0, NCLASS - 1).astype(jnp.int32),
        "down_local": draw_down_local(jax.random.fold_in(keys[16], 71), 0),
        "send_list": draw_send_list(jax.random.fold_in(keys[16], 71), 0),
        "recv_list": draw_recv_list(jax.random.fold_in(keys[16], 71), 0),
        "area_start": jnp.clip(jnp.exp(math.log(2.0) - 2.3025851 * jax.random.uniform(keys[13], (EVENTS, REACHES), jnp.float32) ** levels(keys[13], (EVENTS, REACHES), ((0, 4), (1, 8)), -0.2, 0.2)), 0.2, 2.0),
        "lateral": jnp.clip(jnp.exp(math.log(1.0) - 2.9957323 * jax.random.uniform(keys[14], (STEPS, EVENTS, REACHES), jnp.float32) ** levels(keys[14], (STEPS, EVENTS, REACHES), ((1, 4), (2, 8)), -0.2, 0.2)), 0.05, 1.0),
        "cotangent": bell_draw(keys[15], (EVENTS, REACHES), 1.0, 6.0, ((0, 4), (1, 8)), jnp.float32),
    }


def emit(area_now, flow_rate):
    return flow_rate * area_now ** (5.0 / 3.0)

def advance(area_now, inflow, lateral_now, flow_rate, beta_step):
    return (area_now + beta_step * (inflow + lateral_now)) / (1.0 + beta_step * flow_rate * area_now ** (2.0 / 3.0))

def network_forward(reach_attrs, w_first, b_first, w_second, b_second, w_out):
    tanh_one = jnp.tanh(jnp.dot(reach_attrs, w_first, preferred_element_type=jnp.float32) + b_first)
    hid_one = tanh_one.astype(jnp.bfloat16)
    tanh_two = jnp.tanh(jnp.dot(hid_one, w_second, preferred_element_type=jnp.float32) + b_second)
    hid_two = tanh_two.astype(jnp.bfloat16)
    squash = jax.nn.sigmoid(jnp.dot(hid_two, w_out, preferred_element_type=jnp.float32))
    return (0.02 + 0.08 * squash, (tanh_one, hid_one, tanh_two, hid_two, squash))

def upper_grads(saved_acts, w_out, g_rough, scale):
    tanh_one, hid_one, tanh_two, hid_two, squash = saved_acts
    g_logit = (g_rough * scale * 0.08 * squash * (1.0 - squash)).astype(jnp.bfloat16)
    grad_w_out = jnp.dot(g_logit, hid_two, preferred_element_type=jnp.float32)
    g_pre_two = g_logit.astype(jnp.float32)[:, None] * w_out.astype(jnp.float32)[None, :] * (1.0 - tanh_two * tanh_two)
    g_two = g_pre_two.astype(jnp.bfloat16)
    grad_w_second = jnp.dot(hid_one.T, g_two, preferred_element_type=jnp.float32)
    return (g_two, (grad_w_out, lax.optimization_barrier(jnp.sum(g_pre_two, axis=0)), grad_w_second))

def lower_grads(reach_attrs, w_second, saved_acts, g_two):
    tanh_one = saved_acts[0]
    g_pre_one = jnp.dot(g_two, w_second.T, preferred_element_type=jnp.float32) * (1.0 - tanh_one * tanh_one)
    grad_w_first = jnp.dot(reach_attrs.T, g_pre_one.astype(jnp.bfloat16), preferred_element_type=jnp.float32)
    return (lax.optimization_barrier(jnp.sum(g_pre_one, axis=0)), grad_w_first)

def reference(reach_attrs, w_first, b_first, w_second, b_second, w_out, section_factor, bed_slope, seg_count, section_class, down_local, send_list, recv_list, area_start, lateral, cotangent):
    basins = REACHES // R_DEV
    width_in = reach_attrs.shape[1]
    block_attrs = reach_attrs.reshape(basins, R_DEV, width_in)

    def rough_block(attr_block):
        return network_forward(attr_block, w_first, b_first, w_second, b_second, w_out)[0]
    roughness = lax.map(rough_block, block_attrs).reshape(REACHES)
    one_hot = (section_class[:, None] == jnp.arange(NCLASS, dtype=jnp.int32)[None, :]).astype(jnp.float32)
    k_base = jnp.sqrt(bed_slope) * lax.optimization_barrier(jnp.sum(one_hot * section_factor[None, :], axis=1))
    beta_step = 1.0 / seg_count.astype(jnp.float32)
    owner = jnp.arange(REACHES, dtype=jnp.int32) // R_DEV
    down_global = jnp.where(down_local == R_DEV, REACHES, owner * R_DEV + down_local).astype(jnp.int32)
    source_idx = jnp.arange(basins, dtype=jnp.int32)[:, None, None]
    send_src = jnp.where(send_list == R_DEV, REACHES, source_idx * R_DEV + send_list).astype(jnp.int32).reshape(-1)
    recv_pairs = jnp.transpose(recv_list, (1, 0, 2))
    target_idx = jnp.arange(basins, dtype=jnp.int32)[None, :, None]
    recv_dst = jnp.where(recv_pairs == R_DEV, REACHES, target_idx * R_DEV + recv_pairs).astype(jnp.int32).reshape(-1)

    def confluence(flow_now):
        events_here = flow_now.shape[0]
        padded = jnp.concatenate([flow_now, jnp.zeros((events_here, 1), flow_now.dtype)], axis=1)
        inflow = jnp.zeros((events_here, REACHES + 1), flow_now.dtype).at[:, down_global].add(flow_now)
        inflow = inflow.at[:, recv_dst].add(padded[:, send_src])
        return inflow[:, :REACHES]

    def route(lateral_all, rough_all):
        flow_rate = k_base / rough_all
        area_now = area_start
        flow_now = emit(area_now, flow_rate)
        for step in range(STEPS):
            area_now = advance(area_now, confluence(flow_now), lateral_all[step], flow_rate, beta_step)
            flow_now = emit(area_now, flow_rate)
        return flow_now
    outflow, pull_back = jax.vjp(route, lateral, roughness)
    grad_lateral, g_rough = pull_back(cotangent)
    scale = 32.0 / math.sqrt(EVENTS * REACHES)
    block_grads = g_rough.reshape(basins, R_DEV)

    def add_block(totals, pieces):
        attr_block, g_block = pieces
        saved_acts = network_forward(attr_block, w_first, b_first, w_second, b_second, w_out)[1]
        g_two, upper = upper_grads(saved_acts, w_out, g_block, scale)
        lower = lower_grads(attr_block, w_second, saved_acts, g_two)
        return (jax.tree.map(jnp.add, totals, upper + lower), None)
    start_sums = (jnp.zeros((HID,), jnp.float32), jnp.zeros((HID,), jnp.float32), jnp.zeros((HID, HID), jnp.float32), jnp.zeros((HID,), jnp.float32), jnp.zeros((width_in, HID), jnp.float32))
    totals, _ = lax.scan(add_block, start_sums, (block_attrs, block_grads))
    grad_w_out, grad_b_second, grad_w_second, grad_b_first, grad_w_first = totals
    return (outflow, grad_lateral, grad_w_first, grad_b_first, grad_w_second, grad_b_second, grad_w_out)
```

```python
import functools
import math

import jax
import jax.numpy as jnp
from jax import lax
from jax.experimental import pallas as pl
from jax.experimental.pallas import tpu as pltpu
from jax.sharding import PartitionSpec as P

STEPS = 3
LINKS = 4
GROUP = 32
MESH = pl.DeviceIdType.MESH
NT = (((1,), (1,)), ((), ()))


def split_two(x):
    high = x.astype(jnp.bfloat16)
    low = (x - high.astype(jnp.float32)).astype(jnp.bfloat16)
    return jnp.concatenate([high, low], axis=0)


def kernel(
    n, n_event, owners, chunk, scale,
    w_firstT, w_second, w_secondT, cols, attrs, rows, send_list, recv_list,
    area_start, lateral, cotangent,
    outflow, grad_lateral, full,
    t_one, h_one, d_two, h_two, g_two, squash_row, take_send, take_recv,
    out_msg, in_msg, rate_out, rate_in, slab, rs_in,
    x_send, x_recv, r_send, r_recv, s_send, s_recv, b_send, b_recv, y_send, y_recv, c_send, c_recv,
):
    f32, bf16 = jnp.float32, jnp.bfloat16
    me = lax.axis_index("basin")
    ev = lax.axis_index("event")
    events, reaches = area_start.shape
    hid = w_second.shape[0]
    feat = w_firstT.shape[1]
    part = hid // n_event
    offsets = (1, 2, n // 2, n - 1)
    base = pl.multiple_of(ev * part, 64)

    barrier = pltpu.get_barrier_semaphore()

    @pl.loop(1, n)
    def _(i):
        pl.semaphore_signal(barrier, inc=1, device_id={"basin": lax.rem(me + i, n)}, device_id_type=MESH)

    for i in range(1, n_event):
        pl.semaphore_signal(
            barrier, inc=1, device_id={"event": lax.rem(ev + i, n_event)}, device_id_type=MESH
        )

    tile = 256

    @pl.loop(0, reaches // tile)
    def _(i):
        where = pl.ds(pl.multiple_of(i * tile, tile), tile)
        one = jnp.tanh(
            jnp.dot(w_firstT[...], attrs[0:feat, where], preferred_element_type=f32) + cols[:, 0:1]
        )
        t_one[:, where] = one
        hidden = one.astype(bf16)
        h_one[:, where] = hidden
        two = jnp.tanh(
            jnp.dot(w_secondT[...], hidden, preferred_element_type=f32) + cols[:, 1:2]
        )
        h_two[:, where] = two.astype(bf16)
        d_two[:, where] = cols[:, 2:3] * (1.0 - two * two)
        logit = jnp.sum(two.astype(bf16).astype(f32) * cols[:, 2:3], axis=0, keepdims=True)
        squash_row[:, where] = 1.0 / (1.0 + jnp.exp(-logit))

    slot_row = lax.broadcasted_iota(jnp.int32, (LINKS * GROUP, 1), 0)
    slot = slot_row % GROUP
    cap = send_list.shape[2]
    spread = (
        slot == lax.broadcasted_iota(jnp.int32, (LINKS * GROUP, cap), 1)
    ).astype(f32)
    lane_reach = lax.broadcasted_iota(jnp.int32, (LINKS * GROUP, reaches), 1).astype(f32)
    lane_basin = lax.broadcasted_iota(jnp.int32, (LINKS * GROUP, n), 1)

    def one_hot_of(lists, sign):
        table = lax.dot_general(
            spread, lists[0].astype(f32), NT, precision=lax.Precision.HIGHEST,
            preferred_element_type=f32,
        )
        peer = jnp.zeros((LINKS * GROUP, 1), jnp.int32)
        for k, off in enumerate(offsets):
            peer = jnp.where(slot_row // GROUP == k, lax.rem(me + sign * off + n, n), peer)
        column = jnp.sum(jnp.where(lane_basin == peer, table, 0.0), axis=1, keepdims=True)
        column = jnp.where(slot < cap, column, float(reaches))
        return (jnp.abs(lane_reach - column) < 0.5).astype(bf16)

    take_send[...] = one_hot_of(send_list, 1)
    take_recv[...] = one_hot_of(recv_list, -1)

    squash = squash_row[...]
    rough = 0.02 + 0.08 * squash
    rate = rows[0:1, :] / rough
    beta = rows[1:2, :]
    hop = rows[2:3, :]
    masks = [(jnp.abs(hop - float(d)) < 0.5).astype(f32) for d in range(1, 9)]

    pl.semaphore_wait(barrier, n - 1 + n_event - 1)

    lane_group = lax.broadcasted_iota(jnp.int32, (8, 128), 1) // GROUP
    blocks = events // 8

    def message(index, k, sign):
        return pltpu.make_async_remote_copy(
            src_ref=out_msg.at[index, k],
            dst_ref=in_msg.at[index, k],
            send_sem=x_send.at[index, k],
            recv_sem=x_recv.at[index, k],
            device_id={"basin": lax.rem(me + sign * offsets[k] + n, n)},
            device_id_type=MESH,
        )

    def send(index, field, matrix, sign):
        both = lax.dot_general(split_two(field), matrix[...], NT, preferred_element_type=f32)
        picked = both[:events] + both[events:]
        for k in range(LINKS):
            packed = jnp.zeros((8, 128), f32)
            for q in range(blocks):
                piece = picked[8 * q : 8 * q + 8]
                shift = ((q - k) * GROUP) % 128
                if shift:
                    piece = pltpu.roll(piece, shift, 1)
                packed = jnp.where(lane_group == q, piece, packed)
            out_msg[index, k] = packed
            message(index, k, sign).start()

    def receive(index, matrix, sign):
        for k in range(LINKS):
            message(index, k, sign).wait_recv()
        pieces = []
        for q in range(blocks):
            got = jnp.zeros((8, 128), f32)
            for k in range(LINKS):
                piece = in_msg[index, k]
                shift = ((k - q) * GROUP) % 128
                if shift:
                    piece = pltpu.roll(piece, shift, 1)
                got = jnp.where(lane_group == k, piece, got)
            pieces.append(got)
        both = jnp.dot(
            split_two(jnp.concatenate(pieces, axis=0)), matrix[...], preferred_element_type=f32
        )
        return both[:events] + both[events:]

    def power(area):
        return jnp.exp((2.0 / 3.0) * jnp.log(area))

    areas = [area_start[...]]
    powers = [power(areas[0])]
    shrinks = []
    for t in range(STEPS):
        area, p = areas[t], powers[t]
        flow = rate * area * p
        send(t, flow, take_send, 1)
        inflow = lateral[t]
        for d in range(1, 9):
            inflow = inflow + pltpu.roll(flow * masks[d - 1], d, 1)
        shrink = 1.0 / (1.0 + beta * rate * p)
        shrinks.append(shrink)
        inflow = inflow + receive(t, take_recv, 1)
        areas.append((area + beta * inflow) * shrink)
        powers.append(power(areas[t + 1]))
    emitted = areas[STEPS] * powers[STEPS]
    outflow[...] = rate * emitted
    g_area = cotangent[...] * rate * (5.0 / 3.0) * powers[STEPS]
    g_rate = cotangent[...] * emitted
    for t in reversed(range(STEPS)):
        index = 2 * STEPS - 1 - t
        inner = g_area * shrinks[t]
        g_inflow = inner * beta
        grad_lateral[t] = g_inflow
        send(index, g_inflow, take_recv, -1)
        g_flow = jnp.zeros((events, reaches), f32)
        for d in range(1, 9):
            g_flow = g_flow + masks[d - 1] * pltpu.roll(g_inflow, reaches - d, 1)
        drop = g_inflow * areas[t + 1] * powers[t]
        g_rate = g_rate - drop
        g_area = inner - (2.0 / 3.0) * rate * drop / areas[t]
        g_flow = g_flow + receive(index, take_send, -1)
        g_rate = g_rate + g_flow * areas[t] * powers[t]
        g_area = g_area + (5.0 / 3.0) * rate * powers[t] * g_flow
    rate_out[...] = jnp.sum(g_rate, axis=0, keepdims=True)

    def rate_copy(i):
        return pltpu.make_async_remote_copy(
            src_ref=rate_out,
            dst_ref=rate_in.at[i],
            send_sem=r_send.at[i],
            recv_sem=r_recv.at[i],
            device_id={"event": lax.rem(ev + 1 + i, n_event)},
            device_id_type=MESH,
        )

    for i in range(n_event - 1):
        rate_copy(i).start()
    for i in range(n_event - 1):
        rate_copy(i).wait_recv()
    terms = [rate_out[...]] + [rate_in[i] for i in range(n_event - 1)]
    g_sum = jnp.zeros((1, reaches), f32)
    for e in range(n_event):
        term = terms[0]
        for i in range(n_event - 1):
            term = jnp.where(lax.rem(e + 1 + i, n_event) == ev, terms[i + 1], term)
        g_sum = g_sum + term
    g_logit = (
        g_sum * (-rate / rough) * (scale * 0.08) * squash * (1.0 - squash)
    ).astype(bf16)
    g_logit32 = g_logit.astype(f32)

    @pl.loop(0, hid // 64)
    def _(i):
        where = pl.ds(pl.multiple_of(i * 64, 64), 64)
        g_two[where, :] = (d_two[where, :] * g_logit32).astype(bf16)

    mine = pl.ds(base, part)
    slab[:, 0:hid] = lax.dot_general(h_one[mine, :], g_two[...], NT, preferred_element_type=f32)
    one = t_one[mine, :]
    g_pre = (
        jnp.dot(w_second[mine, :], g_two[...], preferred_element_type=f32) * (1.0 - one * one)
    ).astype(bf16)
    lane_kind = lax.broadcasted_iota(jnp.int32, (128, reaches), 0)
    units = jnp.where(lane_kind == feat + 1, 1.0, 0.0).astype(bf16)
    logits = jnp.where(lane_kind == feat + 2, g_logit32, 0.0).astype(bf16)
    slab[:, hid:] = (
        lax.dot_general(g_pre, attrs[...], NT, preferred_element_type=f32)
        + lax.dot_general(g_two[mine, :], units, NT, preferred_element_type=f32)
        + lax.dot_general(h_two[mine, :], logits, NT, preferred_element_type=f32)
    )

    def when_owner(index, work):
        if owners == n:
            work()
        else:
            pl.when(index < owners)(work)

    def span(index):
        return pl.ds(pl.multiple_of(index * chunk, 8), chunk)

    def scatter_copy(owner, sender):
        return pltpu.make_async_remote_copy(
            src_ref=slab.at[span(owner)],
            dst_ref=rs_in.at[sender],
            send_sem=s_send.at[owner],
            recv_sem=s_recv.at[sender],
            device_id={"basin": owner},
            device_id_type=MESH,
        )

    @pl.loop(1, n)
    def _(i):
        owner = lax.rem(me + i, n)
        when_owner(owner, lambda: scatter_copy(owner, me).start())

    def place(event, index):
        return pl.ds(pl.multiple_of(event * part + index * chunk, 8), chunk)

    def gather_copy(index, peer):
        where = full.at[place(ev, index)]
        return pltpu.make_async_remote_copy(
            src_ref=where, dst_ref=where, send_sem=b_send.at[peer], recv_sem=b_recv.at[index],
            device_id={"basin": peer}, device_id_type=MESH,
        )

    half = lax.rem(ev + n_event // 2, n_event)
    twin = ev + 1 - 2 * lax.rem(ev, 2)
    twin_half = lax.rem(twin + n_event // 2, n_event)

    def half_copy(event, index):
        where = full.at[place(event, index)]
        return pltpu.make_async_remote_copy(
            src_ref=where, dst_ref=where, send_sem=y_send.at[index], recv_sem=y_recv.at[index],
            device_id={"event": half}, device_id_type=MESH,
        )

    def twin_copy(event, index, order):
        where = full.at[place(event, index)]
        return pltpu.make_async_remote_copy(
            src_ref=where, dst_ref=where, send_sem=c_send.at[order, index],
            recv_sem=c_recv.at[order, index],
            device_id={"event": twin}, device_id_type=MESH,
        )

    def own():
        def add(i, total):
            sender = lax.rem(me + n - i, n)
            scatter_copy(me, sender).wait_recv()
            return total + rs_in[sender]

        full[place(ev, me), :] = lax.fori_loop(1, n, add, slab[span(me), :])

        @pl.loop(1, n)
        def _(i):
            gather_copy(me, lax.rem(me + i, n)).start()

        half_copy(ev, me).start()
        twin_copy(ev, me, 0).start()

    when_owner(me, own)

    @pl.loop(1, n)
    def _(i):
        source = lax.rem(me + n - i, n)

        def go():
            gather_copy(source, me).wait_recv()
            half_copy(ev, source).start()
            twin_copy(ev, source, 0).start()

        when_owner(source, go)

    @pl.loop(0, n)
    def _(i):
        source = lax.rem(me + n - i, n)

        def go():
            half_copy(half, source).wait_recv()
            twin_copy(half, source, 1).start()

        when_owner(source, go)

    for index in range(2 * STEPS):
        for k in range(LINKS):
            message(index, k, 1).wait_send()
    for i in range(n_event - 1):
        rate_copy(i).wait_send()

    @pl.loop(1, n)
    def _(i):
        peer = lax.rem(me + i, n)
        when_owner(peer, lambda: scatter_copy(peer, me).wait_send())
        when_owner(me, lambda: gather_copy(me, peer).wait_send())

    @pl.loop(0, owners)
    def _(i):
        half_copy(ev, i).wait_send()
        twin_copy(twin, i, 0).wait_recv()
        twin_copy(twin_half, i, 1).wait_recv()
        twin_copy(ev, i, 0).wait_send()
        twin_copy(half, i, 1).wait_send()


def body(
    n,
    n_event,
    reach_attrs,
    w_first,
    b_first,
    w_second,
    b_second,
    w_out,
    section_factor,
    bed_slope,
    seg_count,
    section_class,
    down_local,
    send_list,
    recv_list,
    area_start,
    lateral,
    cotangent,
):
    f32, bf16 = jnp.float32, jnp.bfloat16
    events, reaches = area_start.shape
    feat, hid = w_first.shape
    class_total = section_factor.shape[0]
    part = hid // n_event
    owners = n if part % (8 * n) == 0 else part // 8
    chunk = part // owners
    scale = 32.0 / math.sqrt(events * n_event * reaches * n)
    one_hot = (section_class[None, :] == jnp.arange(class_total, dtype=jnp.int32)[:, None]).astype(f32)
    k_base = jnp.sqrt(bed_slope) * jnp.sum(one_hot * section_factor[:, None], axis=0)
    position = jnp.arange(reaches, dtype=jnp.int32)
    hop = jnp.where(down_local < reaches, down_local - position, 0).astype(f32)
    rows = jnp.stack([k_base, 1.0 / seg_count.astype(f32), hop], axis=0)
    cols = jnp.stack([b_first, b_second, w_out.astype(f32)], axis=1)
    attrs = jnp.concatenate(
        [reach_attrs.T, jnp.ones((1, reaches), bf16), jnp.zeros((127 - feat, reaches), bf16)], axis=0
    )
    vmem = pl.BlockSpec(memory_space=pltpu.VMEM)
    dma = pltpu.SemaphoreType.DMA
    wide = hid + 128
    outflow, grad_lateral, full = pl.pallas_call(
        functools.partial(kernel, n, n_event, owners, chunk, scale),
        out_shape=(
            jax.ShapeDtypeStruct((events, reaches), f32),
            jax.ShapeDtypeStruct((STEPS, events, reaches), f32),
            jax.ShapeDtypeStruct((hid, wide), f32),
        ),
        in_specs=[vmem] * 11,
        out_specs=(vmem,) * 3,
        scratch_shapes=[
            pltpu.VMEM((hid, reaches), f32),
            pltpu.VMEM((hid, reaches), bf16),
            pltpu.VMEM((hid, reaches), f32),
            pltpu.VMEM((hid, reaches), bf16),
            pltpu.VMEM((hid, reaches), bf16),
            pltpu.VMEM((1, reaches), f32),
            pltpu.VMEM((LINKS * GROUP, reaches), bf16),
            pltpu.VMEM((LINKS * GROUP, reaches), bf16),
            pltpu.VMEM((2 * STEPS, LINKS, 8, 128), f32),
            pltpu.VMEM((2 * STEPS, LINKS, 8, 128), f32),
            pltpu.VMEM((1, reaches), f32),
            pltpu.VMEM((n_event - 1, 1, reaches), f32),
            pltpu.VMEM((part, wide), f32),
            pltpu.VMEM((n, chunk, wide), f32),
            dma((2 * STEPS, LINKS)),
            dma((2 * STEPS, LINKS)),
            dma((n_event - 1,)),
            dma((n_event - 1,)),
            dma((n,)),
            dma((n,)),
            dma((n,)),
            dma((n,)),
            dma((owners,)),
            dma((owners,)),
            dma((2, owners)),
            dma((2, owners)),
        ],
        compiler_params=pltpu.CompilerParams(
            collective_id=0, has_side_effects=True, vmem_limit_bytes=48 * 1024 * 1024
        ),
    )(
        w_first.T, w_second, w_second.T, cols, attrs, rows, send_list, recv_list,
        area_start, lateral, cotangent,
    )
    small = full[:, hid : hid + feat + 3].T
    return (
        outflow,
        grad_lateral,
        small[:feat],
        small[feat],
        full[:, :hid],
        small[feat + 1],
        small[feat + 2],
    )


def solution(mesh):
    return jax.shard_map(
        functools.partial(body, mesh.shape["basin"], mesh.shape["event"]),
        mesh=mesh,
        in_specs=(
            P("basin", None),
            P(),
            P(),
            P(),
            P(),
            P(),
            P(),
            P("basin"),
            P("basin"),
            P("basin"),
            P("basin"),
            P("basin", None, None),
            P("basin", None, None),
            P("event", "basin"),
            P(None, "event", "basin"),
            P("event", "basin"),
        ),
        out_specs=(P("event", "basin"), P(None, "event", "basin"), P(), P(), P(), P(), P()),
        check_vma=False,
    )
```

```python
import functools
import math

import jax
import jax.numpy as jnp
from jax import lax
from jax.experimental import pallas as pl
from jax.experimental.pallas import tpu as pltpu
from jax.sharding import PartitionSpec as P

STEPS = 3
LINKS = 4
GROUP = 32
MESH = pl.DeviceIdType.MESH
NT = (((1,), (1,)), ((), ()))


def split_two(x):
    high = x.astype(jnp.bfloat16)
    low = (x - high.astype(jnp.float32)).astype(jnp.bfloat16)
    return jnp.concatenate([high, low], axis=0)


def kernel(
    n, n_event, owners, chunk, scale,
    w_firstT, w_second, w_secondT, cols, attrs, rows, send_list, recv_list,
    area_start, lateral, cotangent,
    outflow, grad_lateral, full,
    t_one, h_one, d_two, h_two, g_two, squash_row, take_send, take_recv,
    out_msg, in_msg, rate_out, rate_in, slab, rs_pair, rs_line,
    x_send, x_recv, r_send, r_recv, px_send, px_recv, pz_send, pz_recv,
    az_send, az_recv, ax_send, ax_recv, ay_send, ay_recv, ac_send, ac_recv,
    bz_send, bz_recv, bx_send, bx_recv, by_send, by_recv, bc_send, bc_recv,
):
    f32, bf16 = jnp.float32, jnp.bfloat16
    me = lax.axis_index("basin")
    ev = lax.axis_index("event")
    events, reaches = area_start.shape
    hid = w_second.shape[0]
    feat = w_firstT.shape[1]
    part = hid // n_event
    offsets = (1, 2, n // 2, n - 1)
    base = pl.multiple_of(ev * part, 64)

    barrier = pltpu.get_barrier_semaphore()

    @pl.loop(1, n)
    def _(i):
        pl.semaphore_signal(barrier, inc=1, device_id={"basin": lax.rem(me + i, n)}, device_id_type=MESH)

    for i in range(1, n_event):
        pl.semaphore_signal(
            barrier, inc=1, device_id={"event": lax.rem(ev + i, n_event)}, device_id_type=MESH
        )

    tile = 256

    @pl.loop(0, reaches // tile)
    def _(i):
        where = pl.ds(pl.multiple_of(i * tile, tile), tile)
        one = jnp.tanh(
            jnp.dot(w_firstT[...], attrs[0:feat, where], preferred_element_type=f32) + cols[:, 0:1]
        )
        t_one[:, where] = one
        hidden = one.astype(bf16)
        h_one[:, where] = hidden
        two = jnp.tanh(
            jnp.dot(w_secondT[...], hidden, preferred_element_type=f32) + cols[:, 1:2]
        )
        h_two[:, where] = two.astype(bf16)
        d_two[:, where] = cols[:, 2:3] * (1.0 - two * two)
        logit = jnp.sum(two.astype(bf16).astype(f32) * cols[:, 2:3], axis=0, keepdims=True)
        squash_row[:, where] = 1.0 / (1.0 + jnp.exp(-logit))

    slot_row = lax.broadcasted_iota(jnp.int32, (LINKS * GROUP, 1), 0)
    slot = slot_row % GROUP
    cap = send_list.shape[2]
    spread = (
        slot == lax.broadcasted_iota(jnp.int32, (LINKS * GROUP, cap), 1)
    ).astype(f32)
    lane_reach = lax.broadcasted_iota(jnp.int32, (LINKS * GROUP, reaches), 1).astype(f32)
    lane_basin = lax.broadcasted_iota(jnp.int32, (LINKS * GROUP, n), 1)

    def one_hot_of(lists, sign):
        table = lax.dot_general(
            spread, lists[0].astype(f32), NT, precision=lax.Precision.HIGHEST,
            preferred_element_type=f32,
        )
        peer = jnp.zeros((LINKS * GROUP, 1), jnp.int32)
        for k, off in enumerate(offsets):
            peer = jnp.where(slot_row // GROUP == k, lax.rem(me + sign * off + n, n), peer)
        column = jnp.sum(jnp.where(lane_basin == peer, table, 0.0), axis=1, keepdims=True)
        column = jnp.where(slot < cap, column, float(reaches))
        return (jnp.abs(lane_reach - column) < 0.5).astype(bf16)

    take_send[...] = one_hot_of(send_list, 1)
    take_recv[...] = one_hot_of(recv_list, -1)

    squash = squash_row[...]
    rough = 0.02 + 0.08 * squash
    rate = rows[0:1, :] / rough
    beta = rows[1:2, :]
    hop = rows[2:3, :]
    masks = [(jnp.abs(hop - float(d)) < 0.5).astype(f32) for d in range(1, 9)]

    pl.semaphore_wait(barrier, n - 1 + n_event - 1)

    lane_group = lax.broadcasted_iota(jnp.int32, (8, 128), 1) // GROUP
    blocks = events // 8

    def message(index, k, sign):
        return pltpu.make_async_remote_copy(
            src_ref=out_msg.at[index, k],
            dst_ref=in_msg.at[index, k],
            send_sem=x_send.at[index, k],
            recv_sem=x_recv.at[index, k],
            device_id={"basin": lax.rem(me + sign * offsets[k] + n, n)},
            device_id_type=MESH,
        )

    def send(index, field, matrix, sign):
        both = lax.dot_general(split_two(field), matrix[...], NT, preferred_element_type=f32)
        picked = both[:events] + both[events:]
        for k in range(LINKS):
            packed = jnp.zeros((8, 128), f32)
            for q in range(blocks):
                piece = picked[8 * q : 8 * q + 8]
                shift = ((q - k) * GROUP) % 128
                if shift:
                    piece = pltpu.roll(piece, shift, 1)
                packed = jnp.where(lane_group == q, piece, packed)
            out_msg[index, k] = packed
            message(index, k, sign).start()

    def receive(index, matrix, sign):
        for k in range(LINKS):
            message(index, k, sign).wait_recv()
        pieces = []
        for q in range(blocks):
            got = jnp.zeros((8, 128), f32)
            for k in range(LINKS):
                piece = in_msg[index, k]
                shift = ((k - q) * GROUP) % 128
                if shift:
                    piece = pltpu.roll(piece, shift, 1)
                got = jnp.where(lane_group == k, piece, got)
            pieces.append(got)
        both = jnp.dot(
            split_two(jnp.concatenate(pieces, axis=0)), matrix[...], preferred_element_type=f32
        )
        return both[:events] + both[events:]

    def power(area):
        return jnp.exp((2.0 / 3.0) * jnp.log(area))

    areas = [area_start[...]]
    powers = [power(areas[0])]
    shrinks = []
    for t in range(STEPS):
        area, p = areas[t], powers[t]
        flow = rate * area * p
        send(t, flow, take_send, 1)
        inflow = lateral[t]
        for d in range(1, 9):
            inflow = inflow + pltpu.roll(flow * masks[d - 1], d, 1)
        shrink = 1.0 / (1.0 + beta * rate * p)
        shrinks.append(shrink)
        inflow = inflow + receive(t, take_recv, 1)
        areas.append((area + beta * inflow) * shrink)
        powers.append(power(areas[t + 1]))
    emitted = areas[STEPS] * powers[STEPS]
    outflow[...] = rate * emitted
    g_area = cotangent[...] * rate * (5.0 / 3.0) * powers[STEPS]
    g_rate = cotangent[...] * emitted
    for t in reversed(range(STEPS)):
        index = 2 * STEPS - 1 - t
        inner = g_area * shrinks[t]
        g_inflow = inner * beta
        grad_lateral[t] = g_inflow
        send(index, g_inflow, take_recv, -1)
        g_flow = jnp.zeros((events, reaches), f32)
        for d in range(1, 9):
            g_flow = g_flow + masks[d - 1] * pltpu.roll(g_inflow, reaches - d, 1)
        drop = g_inflow * areas[t + 1] * powers[t]
        g_rate = g_rate - drop
        g_area = inner - (2.0 / 3.0) * rate * drop / areas[t]
        g_flow = g_flow + receive(index, take_send, -1)
        g_rate = g_rate + g_flow * areas[t] * powers[t]
        g_area = g_area + (5.0 / 3.0) * rate * powers[t] * g_flow
    rate_out[...] = jnp.sum(g_rate, axis=0, keepdims=True)

    def rate_copy(i):
        return pltpu.make_async_remote_copy(
            src_ref=rate_out,
            dst_ref=rate_in.at[i],
            send_sem=r_send.at[i],
            recv_sem=r_recv.at[i],
            device_id={"event": lax.rem(ev + 1 + i, n_event)},
            device_id_type=MESH,
        )

    for i in range(n_event - 1):
        rate_copy(i).start()
    for i in range(n_event - 1):
        rate_copy(i).wait_recv()
    terms = [rate_out[...]] + [rate_in[i] for i in range(n_event - 1)]
    g_sum = jnp.zeros((1, reaches), f32)
    for e in range(n_event):
        term = terms[0]
        for i in range(n_event - 1):
            term = jnp.where(lax.rem(e + 1 + i, n_event) == ev, terms[i + 1], term)
        g_sum = g_sum + term
    g_logit = (
        g_sum * (-rate / rough) * (scale * 0.08) * squash * (1.0 - squash)
    ).astype(bf16)
    g_logit32 = g_logit.astype(f32)

    @pl.loop(0, hid // 64)
    def _(i):
        where = pl.ds(pl.multiple_of(i * 64, 64), 64)
        g_two[where, :] = (d_two[where, :] * g_logit32).astype(bf16)

    mine = pl.ds(base, part)
    slab[:, 0:hid] = lax.dot_general(h_one[mine, :], g_two[...], NT, preferred_element_type=f32)
    one = t_one[mine, :]
    g_pre = (
        jnp.dot(w_second[mine, :], g_two[...], preferred_element_type=f32) * (1.0 - one * one)
    ).astype(bf16)
    lane_kind = lax.broadcasted_iota(jnp.int32, (128, reaches), 0)
    units = jnp.where(lane_kind == feat + 1, 1.0, 0.0).astype(bf16)
    logits = jnp.where(lane_kind == feat + 2, g_logit32, 0.0).astype(bf16)
    slab[:, hid:] = (
        lax.dot_general(g_pre, attrs[...], NT, preferred_element_type=f32)
        + lax.dot_general(g_two[mine, :], units, NT, preferred_element_type=f32)
        + lax.dot_general(h_two[mine, :], logits, NT, preferred_element_type=f32)
    )

    def when_owner(index, work):
        if owners == n:
            work()
        else:
            pl.when(index < owners)(work)

    def span(index):
        return pl.ds(pl.multiple_of(index * chunk, 8), chunk)

    line = n // 2
    low = lax.rem(me, 2)
    spot = me // 2
    pair = me + 1 - 2 * low
    half = lax.rem(ev + n_event // 2, n_event)
    twin = ev + 1 - 2 * lax.rem(ev, 2)
    twin_half = lax.rem(twin + n_event // 2, n_event)

    def device(z, parity):
        return 2 * z + parity

    def pair_sum(z, parity):
        return pltpu.make_async_remote_copy(
            src_ref=slab.at[span(device(z, parity))], dst_ref=rs_pair.at[z],
            send_sem=px_send.at[z], recv_sem=px_recv.at[z],
            device_id={"basin": pair}, device_id_type=MESH,
        )

    def line_sum(z, sender):
        return pltpu.make_async_remote_copy(
            src_ref=rs_pair.at[z], dst_ref=rs_line.at[sender],
            send_sem=pz_send.at[z], recv_sem=pz_recv.at[sender],
            device_id={"basin": device(z, low)}, device_id_type=MESH,
        )

    for j in range(line):
        z = lax.rem(spot + 1 + j, line)
        when_owner(device(z, 1 - low), lambda z=z: pair_sum(z, 1 - low).start())

    @pl.loop(0, line)
    def _(j):
        z = lax.rem(spot + 1 + j, line)

        def go():
            pair_sum(z, 1 - low).wait_recv()
            rs_pair[z] = rs_pair[z] + slab[span(device(z, low)), :]

            @pl.when(j < line - 1)
            def _():
                line_sum(z, spot).start()

        when_owner(device(z, low), go)

    late = chunk if chunk < 24 else chunk // 24 * 16
    early = chunk - late

    def rows_a(event, z, parity):
        return full.at[pl.ds(pl.multiple_of(event * part + device(z, parity) * chunk, 8), late)]

    def rows_b(event, z, parity):
        start = event * part + device(z, parity) * chunk + late
        return full.at[pl.ds(pl.multiple_of(start, 8), early)]

    def move(where, send_sem, recv_sem, target):
        return pltpu.make_async_remote_copy(
            src_ref=where, dst_ref=where, send_sem=send_sem, recv_sem=recv_sem,
            device_id=target, device_id_type=MESH,
        )

    def a_line(source, peer):
        return move(rows_a(ev, source, low), az_send.at[peer], az_recv.at[source],
                    {"basin": device(peer, low)})

    def a_pair(z, parity):
        return move(rows_a(ev, z, parity), ax_send.at[z], ax_recv.at[z], {"basin": pair})

    def a_half(event, z, parity):
        at = device(z, parity)
        return move(rows_a(event, z, parity), ay_send.at[at], ay_recv.at[at], {"event": half})

    def a_twin(side, event, z, parity):
        at = device(z, parity)
        return move(rows_a(event, z, parity), ac_send.at[side, at], ac_recv.at[side, at],
                    {"event": twin})

    def b_line(side, source, peer):
        return move(rows_b((ev, half)[side], source, low), bz_send.at[side, peer],
                    bz_recv.at[side, source], {"basin": device(peer, low)})

    def b_pair(side, z, parity):
        return move(rows_b((ev, half)[side], z, parity), bx_send.at[side, z],
                    bx_recv.at[side, z], {"basin": pair})

    def b_half(event):
        return move(rows_b(event, spot, low), by_send, by_recv, {"event": half})

    def b_twin(side, event, z, parity):
        at = device(z, parity)
        return move(rows_b(event, z, parity), bc_send.at[side, at], bc_recv.at[side, at],
                    {"event": twin})

    def a_on(z, parity):
        a_half(ev, z, parity).start()
        a_twin(0, ev, z, parity).start()

    def b_spread(side):
        for j in range(1, line):
            b_line(side, spot, lax.rem(spot + j, line)).start()
        b_pair(side, spot, low).start()
        b_twin(side, (ev, half)[side], spot, low).start()

    def own():
        def add(i, total):
            sender = lax.rem(spot + line - i, line)
            line_sum(spot, sender).wait_recv()
            return total + rs_line[sender]

        full[pl.ds(pl.multiple_of(ev * part + me * chunk, 8), chunk), :] = lax.fori_loop(
            1, line, add, rs_pair[spot]
        )

        a_half(ev, spot, low).start()
        for j in range(1, line):
            a_line(spot, lax.rem(spot + j, line)).start()
        a_pair(spot, low).start()
        a_twin(0, ev, spot, low).start()
        if early:
            b_half(ev).start()
            b_spread(0)

    when_owner(me, own)
    when_owner(pair, lambda: (a_pair(spot, 1 - low).wait_recv(), a_on(spot, 1 - low))[0])
    if early:
        b_half(half).wait_recv()
        b_spread(1)

    @pl.loop(1, line)
    def _(j):
        z = lax.rem(spot + line - j, line)

        def go():
            a_line(z, spot).wait_recv()
            a_half(ev, z, low).start()
            a_pair(z, low).start()
            a_twin(0, ev, z, low).start()

        when_owner(device(z, low), go)

        def go_pair():
            a_pair(z, 1 - low).wait_recv()
            a_on(z, 1 - low)

        when_owner(device(z, 1 - low), go_pair)

    if early:
        for side in range(2):
            event = (ev, half)[side]
            b_pair(side, spot, 1 - low).wait_recv()
            b_twin(side, event, spot, 1 - low).start()

        @pl.loop(1, line)
        def _(j):
            z = lax.rem(spot + line - j, line)
            for side in range(2):
                event = (ev, half)[side]
                b_line(side, z, spot).wait_recv()
                b_pair(side, z, low).start()
                b_twin(side, event, z, low).start()
            for side in range(2):
                event = (ev, half)[side]
                b_pair(side, z, 1 - low).wait_recv()
                b_twin(side, event, z, 1 - low).start()

    @pl.loop(0, line)
    def _(j):
        z = lax.rem(spot + line - j, line)
        for parity in (low, 1 - low):

            def go():
                a_half(half, z, parity).wait_recv()
                a_twin(1, half, z, parity).start()

            when_owner(device(z, parity), go)

    for index in range(2 * STEPS):
        for k in range(LINKS):
            message(index, k, 1).wait_send()
    for i in range(n_event - 1):
        rate_copy(i).wait_send()

    @pl.loop(0, line)
    def _(z):
        when_owner(device(z, 1 - low), lambda: pair_sum(z, 1 - low).wait_send())
        when_owner(device(z, low), lambda: a_pair(z, low).wait_send())

        @pl.when(z != spot)
        def _():
            when_owner(device(z, low), lambda: line_sum(z, spot).wait_send())
            when_owner(me, lambda: a_line(spot, z).wait_send())

        if early:
            for side in range(2):
                b_pair(side, z, low).wait_send()

                @pl.when(z != spot)
                def _():
                    b_line(side, spot, z).wait_send()

        for parity in range(2):

            def go():
                a_half(ev, z, parity).wait_send()
                a_twin(0, twin, z, parity).wait_recv()
                a_twin(1, twin_half, z, parity).wait_recv()
                a_twin(0, ev, z, parity).wait_send()
                a_twin(1, half, z, parity).wait_send()
                if early:
                    for side in range(2):
                        b_twin(side, (twin, twin_half)[side], z, parity).wait_recv()
                        b_twin(side, (ev, half)[side], z, parity).wait_send()

            when_owner(device(z, parity), go)

    if early:
        b_half(ev).wait_send()


def body(
    n,
    n_event,
    reach_attrs,
    w_first,
    b_first,
    w_second,
    b_second,
    w_out,
    section_factor,
    bed_slope,
    seg_count,
    section_class,
    down_local,
    send_list,
    recv_list,
    area_start,
    lateral,
    cotangent,
):
    f32, bf16 = jnp.float32, jnp.bfloat16
    events, reaches = area_start.shape
    feat, hid = w_first.shape
    class_total = section_factor.shape[0]
    part = hid // n_event
    owners = n if part % (8 * n) == 0 else part // 8
    chunk = part // owners
    scale = 32.0 / math.sqrt(events * n_event * reaches * n)
    one_hot = (section_class[None, :] == jnp.arange(class_total, dtype=jnp.int32)[:, None]).astype(f32)
    k_base = jnp.sqrt(bed_slope) * jnp.sum(one_hot * section_factor[:, None], axis=0)
    position = jnp.arange(reaches, dtype=jnp.int32)
    hop = jnp.where(down_local < reaches, down_local - position, 0).astype(f32)
    rows = jnp.stack([k_base, 1.0 / seg_count.astype(f32), hop], axis=0)
    cols = jnp.stack([b_first, b_second, w_out.astype(f32)], axis=1)
    attrs = jnp.concatenate(
        [reach_attrs.T, jnp.ones((1, reaches), bf16), jnp.zeros((127 - feat, reaches), bf16)], axis=0
    )
    vmem = pl.BlockSpec(memory_space=pltpu.VMEM)
    dma = pltpu.SemaphoreType.DMA
    wide = hid + 128
    outflow, grad_lateral, full = pl.pallas_call(
        functools.partial(kernel, n, n_event, owners, chunk, scale),
        out_shape=(
            jax.ShapeDtypeStruct((events, reaches), f32),
            jax.ShapeDtypeStruct((STEPS, events, reaches), f32),
            jax.ShapeDtypeStruct((hid, wide), f32),
        ),
        in_specs=[vmem] * 11,
        out_specs=(vmem,) * 3,
        scratch_shapes=[
            pltpu.VMEM((hid, reaches), f32),
            pltpu.VMEM((hid, reaches), bf16),
            pltpu.VMEM((hid, reaches), f32),
            pltpu.VMEM((hid, reaches), bf16),
            pltpu.VMEM((hid, reaches), bf16),
            pltpu.VMEM((1, reaches), f32),
            pltpu.VMEM((LINKS * GROUP, reaches), bf16),
            pltpu.VMEM((LINKS * GROUP, reaches), bf16),
            pltpu.VMEM((2 * STEPS, LINKS, 8, 128), f32),
            pltpu.VMEM((2 * STEPS, LINKS, 8, 128), f32),
            pltpu.VMEM((1, reaches), f32),
            pltpu.VMEM((n_event - 1, 1, reaches), f32),
            pltpu.VMEM((part, wide), f32),
            pltpu.VMEM((n // 2, chunk, wide), f32),
            pltpu.VMEM((n // 2, chunk, wide), f32),
            dma((2 * STEPS, LINKS)),
            dma((2 * STEPS, LINKS)),
            dma((n_event - 1,)),
            dma((n_event - 1,)),
            dma((n // 2,)),
            dma((n // 2,)),
            dma((n // 2,)),
            dma((n // 2,)),
            dma((n // 2,)),
            dma((n // 2,)),
            dma((n // 2,)),
            dma((n // 2,)),
            dma((n,)),
            dma((n,)),
            dma((2, n)),
            dma((2, n)),
            dma((2, n // 2)),
            dma((2, n // 2)),
            dma((2, n // 2)),
            dma((2, n // 2)),
            dma,
            dma,
            dma((2, n)),
            dma((2, n)),
        ],
        compiler_params=pltpu.CompilerParams(
            collective_id=0, has_side_effects=True, vmem_limit_bytes=48 * 1024 * 1024
        ),
    )(
        w_first.T, w_second, w_second.T, cols, attrs, rows, send_list, recv_list,
        area_start, lateral, cotangent,
    )
    small = full[:, hid : hid + feat + 3].T
    return (
        outflow,
        grad_lateral,
        small[:feat],
        small[feat],
        full[:, :hid],
        small[feat + 1],
        small[feat + 2],
    )


def solution(mesh):
    return jax.shard_map(
        functools.partial(body, mesh.shape["basin"], mesh.shape["event"]),
        mesh=mesh,
        in_specs=(
            P("basin", None),
            P(),
            P(),
            P(),
            P(),
            P(),
            P(),
            P("basin"),
            P("basin"),
            P("basin"),
            P("basin"),
            P("basin", None, None),
            P("basin", None, None),
            P("event", "basin"),
            P(None, "event", "basin"),
            P("event", "basin"),
        ),
        out_specs=(P("event", "basin"), P(None, "event", "basin"), P(), P(), P(), P(), P()),
        check_vma=False,
    )
```

```python
import functools
import math

import jax
import jax.numpy as jnp
from jax import lax
from jax.experimental import pallas as pl
from jax.experimental.pallas import tpu as pltpu
from jax.sharding import PartitionSpec as P

STEPS = 3
LINKS = 4
GROUP = 32
MESH = pl.DeviceIdType.MESH
NT = (((1,), (1,)), ((), ()))


def split_two(x):
    high = x.astype(jnp.bfloat16)
    low = (x - high.astype(jnp.float32)).astype(jnp.bfloat16)
    return jnp.concatenate([high, low], axis=0)


def kernel(
    n, n_event, owners, chunk, scale,
    w_firstT, w_second, w_secondT, cols, attrs, rows, send_list, recv_list,
    area_start, lateral, cotangent,
    outflow, grad_lateral, full,
    t_one, h_one, d_two, h_two, g_two, squash_row, take_send, take_recv,
    out_msg, in_msg, rate_out, rate_in, slab, rs_pair, rs_line,
    x_send, x_recv, r_send, r_recv, px_send, px_recv, pz_send, pz_recv,
    az_send, az_recv, ax_send, ax_recv, ay_send, ay_recv, ac_send, ac_recv,
    bz_send, bz_recv, bx_send, bx_recv, by_send, by_recv, bc_send, bc_recv,
):
    f32, bf16 = jnp.float32, jnp.bfloat16
    me = lax.axis_index("basin")
    ev = lax.axis_index("event")
    events, reaches = area_start.shape
    hid = w_second.shape[0]
    feat = w_firstT.shape[1]
    part = hid // n_event
    offsets = (1, 2, n // 2, n - 1)
    base = pl.multiple_of(ev * part, 64)

    barrier = pltpu.get_barrier_semaphore()

    @pl.loop(1, n)
    def _(i):
        pl.semaphore_signal(barrier, inc=1, device_id={"basin": lax.rem(me + i, n)}, device_id_type=MESH)

    for i in range(1, n_event):
        pl.semaphore_signal(
            barrier, inc=1, device_id={"event": lax.rem(ev + i, n_event)}, device_id_type=MESH
        )

    tile = 256

    @pl.loop(0, reaches // tile)
    def _(i):
        where = pl.ds(pl.multiple_of(i * tile, tile), tile)
        one = jnp.tanh(
            jnp.dot(w_firstT[...], attrs[0:feat, where], preferred_element_type=f32) + cols[:, 0:1]
        )
        t_one[:, where] = one
        hidden = one.astype(bf16)
        h_one[:, where] = hidden
        two = jnp.tanh(
            jnp.dot(w_secondT[...], hidden, preferred_element_type=f32) + cols[:, 1:2]
        )
        h_two[:, where] = two.astype(bf16)
        d_two[:, where] = cols[:, 2:3] * (1.0 - two * two)
        logit = jnp.sum(two.astype(bf16).astype(f32) * cols[:, 2:3], axis=0, keepdims=True)
        squash_row[:, where] = 1.0 / (1.0 + jnp.exp(-logit))

    slot_row = lax.broadcasted_iota(jnp.int32, (LINKS * GROUP, 1), 0)
    slot = slot_row % GROUP
    cap = send_list.shape[2]
    spread = (
        slot == lax.broadcasted_iota(jnp.int32, (LINKS * GROUP, cap), 1)
    ).astype(f32)
    lane_reach = lax.broadcasted_iota(jnp.int32, (LINKS * GROUP, reaches), 1).astype(f32)
    lane_basin = lax.broadcasted_iota(jnp.int32, (LINKS * GROUP, n), 1)

    def one_hot_of(lists, sign):
        table = lax.dot_general(
            spread, lists[0].astype(f32), NT, precision=lax.Precision.HIGHEST,
            preferred_element_type=f32,
        )
        peer = jnp.zeros((LINKS * GROUP, 1), jnp.int32)
        for k, off in enumerate(offsets):
            peer = jnp.where(slot_row // GROUP == k, lax.rem(me + sign * off + n, n), peer)
        column = jnp.sum(jnp.where(lane_basin == peer, table, 0.0), axis=1, keepdims=True)
        column = jnp.where(slot < cap, column, float(reaches))
        return (jnp.abs(lane_reach - column) < 0.5).astype(bf16)

    take_send[...] = one_hot_of(send_list, 1)
    take_recv[...] = one_hot_of(recv_list, -1)

    squash = squash_row[...]
    rough = 0.02 + 0.08 * squash
    rate = rows[0:1, :] / rough
    beta = rows[1:2, :]
    hop = rows[2:3, :]
    masks = [(jnp.abs(hop - float(d)) < 0.5).astype(f32) for d in range(1, 9)]

    pl.semaphore_wait(barrier, n - 1 + n_event - 1)

    lane_group = lax.broadcasted_iota(jnp.int32, (8, 128), 1) // GROUP
    blocks = events // 8

    def message(index, k, sign):
        return pltpu.make_async_remote_copy(
            src_ref=out_msg.at[index, k],
            dst_ref=in_msg.at[index, k],
            send_sem=x_send.at[index, k],
            recv_sem=x_recv.at[index, k],
            device_id={"basin": lax.rem(me + sign * offsets[k] + n, n)},
            device_id_type=MESH,
        )

    def send(index, field, matrix, sign):
        both = lax.dot_general(split_two(field), matrix[...], NT, preferred_element_type=f32)
        picked = both[:events] + both[events:]
        for k in range(LINKS):
            packed = jnp.zeros((8, 128), f32)
            for q in range(blocks):
                piece = picked[8 * q : 8 * q + 8]
                shift = ((q - k) * GROUP) % 128
                if shift:
                    piece = pltpu.roll(piece, shift, 1)
                packed = jnp.where(lane_group == q, piece, packed)
            out_msg[index, k] = packed
            message(index, k, sign).start()

    def receive(index, matrix, sign):
        for k in range(LINKS):
            message(index, k, sign).wait_recv()
        pieces = []
        for q in range(blocks):
            got = jnp.zeros((8, 128), f32)
            for k in range(LINKS):
                piece = in_msg[index, k]
                shift = ((k - q) * GROUP) % 128
                if shift:
                    piece = pltpu.roll(piece, shift, 1)
                got = jnp.where(lane_group == k, piece, got)
            pieces.append(got)
        both = jnp.dot(
            split_two(jnp.concatenate(pieces, axis=0)), matrix[...], preferred_element_type=f32
        )
        return both[:events] + both[events:]

    def power(area):
        return jnp.exp((2.0 / 3.0) * jnp.log(area))

    areas = [area_start[...]]
    powers = [power(areas[0])]
    shrinks = []
    for t in range(STEPS):
        area, p = areas[t], powers[t]
        flow = rate * area * p
        send(t, flow, take_send, 1)
        inflow = lateral[t]
        for d in range(1, 9):
            inflow = inflow + pltpu.roll(flow * masks[d - 1], d, 1)
        shrink = 1.0 / (1.0 + beta * rate * p)
        shrinks.append(shrink)
        inflow = inflow + receive(t, take_recv, 1)
        areas.append((area + beta * inflow) * shrink)
        powers.append(power(areas[t + 1]))
    emitted = areas[STEPS] * powers[STEPS]
    outflow[...] = rate * emitted
    g_area = cotangent[...] * rate * (5.0 / 3.0) * powers[STEPS]
    g_rate = cotangent[...] * emitted
    for t in reversed(range(STEPS)):
        index = 2 * STEPS - 1 - t
        inner = g_area * shrinks[t]
        g_inflow = inner * beta
        grad_lateral[t] = g_inflow
        send(index, g_inflow, take_recv, -1)
        g_flow = jnp.zeros((events, reaches), f32)
        for d in range(1, 9):
            g_flow = g_flow + masks[d - 1] * pltpu.roll(g_inflow, reaches - d, 1)
        drop = g_inflow * areas[t + 1] * powers[t]
        g_rate = g_rate - drop
        g_area = inner - (2.0 / 3.0) * rate * drop / areas[t]
        g_flow = g_flow + receive(index, take_send, -1)
        g_rate = g_rate + g_flow * areas[t] * powers[t]
        g_area = g_area + (5.0 / 3.0) * rate * powers[t] * g_flow
    rate_out[...] = jnp.sum(g_rate, axis=0, keepdims=True)

    def rate_copy(i):
        return pltpu.make_async_remote_copy(
            src_ref=rate_out,
            dst_ref=rate_in.at[i],
            send_sem=r_send.at[i],
            recv_sem=r_recv.at[i],
            device_id={"event": lax.rem(ev + 1 + i, n_event)},
            device_id_type=MESH,
        )

    for i in range(n_event - 1):
        rate_copy(i).start()
    for i in range(n_event - 1):
        rate_copy(i).wait_recv()
    terms = [rate_out[...]] + [rate_in[i] for i in range(n_event - 1)]
    g_sum = jnp.zeros((1, reaches), f32)
    for e in range(n_event):
        term = terms[0]
        for i in range(n_event - 1):
            term = jnp.where(lax.rem(e + 1 + i, n_event) == ev, terms[i + 1], term)
        g_sum = g_sum + term
    g_logit = (
        g_sum * (-rate / rough) * (scale * 0.08) * squash * (1.0 - squash)
    ).astype(bf16)
    g_logit32 = g_logit.astype(f32)

    @pl.loop(0, hid // 64)
    def _(i):
        where = pl.ds(pl.multiple_of(i * 64, 64), 64)
        g_two[where, :] = (d_two[where, :] * g_logit32).astype(bf16)

    mine = pl.ds(base, part)
    slab[:, 0:hid] = lax.dot_general(h_one[mine, :], g_two[...], NT, preferred_element_type=f32)
    one = t_one[mine, :]
    g_pre = (
        jnp.dot(w_second[mine, :], g_two[...], preferred_element_type=f32) * (1.0 - one * one)
    ).astype(bf16)
    lane_kind = lax.broadcasted_iota(jnp.int32, (128, reaches), 0)
    units = jnp.where(lane_kind == feat + 1, 1.0, 0.0).astype(bf16)
    logits = jnp.where(lane_kind == feat + 2, g_logit32, 0.0).astype(bf16)
    slab[:, hid:] = (
        lax.dot_general(g_pre, attrs[...], NT, preferred_element_type=f32)
        + lax.dot_general(g_two[mine, :], units, NT, preferred_element_type=f32)
        + lax.dot_general(h_two[mine, :], logits, NT, preferred_element_type=f32)
    )

    def when_owner(index, work):
        if owners == n:
            work()
        else:
            pl.when(index < owners)(work)

    def span(index):
        return pl.ds(pl.multiple_of(index * chunk, 8), chunk)

    line = n // 2
    low = lax.rem(me, 2)
    spot = me // 2
    pair = me + 1 - 2 * low
    half = lax.rem(ev + n_event // 2, n_event)
    twin = ev + 1 - 2 * lax.rem(ev, 2)
    twin_half = lax.rem(twin + n_event // 2, n_event)

    def device(z, parity):
        return 2 * z + parity

    def pair_sum(z, parity):
        return pltpu.make_async_remote_copy(
            src_ref=slab.at[span(device(z, parity))], dst_ref=rs_pair.at[z],
            send_sem=px_send.at[z], recv_sem=px_recv.at[z],
            device_id={"basin": pair}, device_id_type=MESH,
        )

    def line_sum(z, sender):
        return pltpu.make_async_remote_copy(
            src_ref=rs_pair.at[z], dst_ref=rs_line.at[sender],
            send_sem=pz_send.at[z], recv_sem=pz_recv.at[sender],
            device_id={"basin": device(z, low)}, device_id_type=MESH,
        )

    for j in range(line):
        z = lax.rem(spot + 1 + j, line)
        when_owner(device(z, 1 - low), lambda z=z: pair_sum(z, 1 - low).start())

    @pl.loop(0, line)
    def _(j):
        z = lax.rem(spot + 1 + j, line)

        def go():
            pair_sum(z, 1 - low).wait_recv()
            rs_pair[z] = rs_pair[z] + slab[span(device(z, low)), :]

            @pl.when(j < line - 1)
            def _():
                line_sum(z, spot).start()

        when_owner(device(z, low), go)

    early = 0
    late = chunk - early

    def rows_a(event, z, parity):
        return full.at[pl.ds(pl.multiple_of(event * part + device(z, parity) * chunk, 8), late)]

    def rows_b(event, z, parity):
        start = event * part + device(z, parity) * chunk + late
        return full.at[pl.ds(pl.multiple_of(start, 8), early)]

    def move(where, send_sem, recv_sem, target):
        return pltpu.make_async_remote_copy(
            src_ref=where, dst_ref=where, send_sem=send_sem, recv_sem=recv_sem,
            device_id=target, device_id_type=MESH,
        )

    def a_line(source, peer):
        return move(rows_a(ev, source, low), az_send.at[peer], az_recv.at[source],
                    {"basin": device(peer, low)})

    def a_pair(z, parity):
        return move(rows_a(ev, z, parity), ax_send.at[z], ax_recv.at[z], {"basin": pair})

    def a_half(event, z, parity):
        at = device(z, parity)
        return move(rows_a(event, z, parity), ay_send.at[at], ay_recv.at[at], {"event": half})

    def a_twin(side, event, z, parity):
        at = device(z, parity)
        return move(rows_a(event, z, parity), ac_send.at[side, at], ac_recv.at[side, at],
                    {"event": twin})

    def b_line(side, source, peer):
        return move(rows_b((ev, half)[side], source, low), bz_send.at[side, peer],
                    bz_recv.at[side, source], {"basin": device(peer, low)})

    def b_pair(side, z, parity):
        return move(rows_b((ev, half)[side], z, parity), bx_send.at[side, z],
                    bx_recv.at[side, z], {"basin": pair})

    def b_half(event):
        return move(rows_b(event, spot, low), by_send, by_recv, {"event": half})

    def b_twin(side, event, z, parity):
        at = device(z, parity)
        return move(rows_b(event, z, parity), bc_send.at[side, at], bc_recv.at[side, at],
                    {"event": twin})

    def a_on(z, parity):
        a_half(ev, z, parity).start()
        a_twin(0, ev, z, parity).start()

    def b_spread(side):
        for j in range(1, line):
            b_line(side, spot, lax.rem(spot + j, line)).start()
        b_pair(side, spot, low).start()
        b_twin(side, (ev, half)[side], spot, low).start()

    def own():
        def add(i, total):
            sender = lax.rem(spot + line - i, line)
            line_sum(spot, sender).wait_recv()
            return total + rs_line[sender]

        full[pl.ds(pl.multiple_of(ev * part + me * chunk, 8), chunk), :] = lax.fori_loop(
            1, line, add, rs_pair[spot]
        )

        a_half(ev, spot, low).start()
        for j in range(1, line):
            a_line(spot, lax.rem(spot + j, line)).start()
        a_pair(spot, low).start()
        a_twin(0, ev, spot, low).start()
        if early:
            b_half(ev).start()
            b_spread(0)

    when_owner(me, own)
    when_owner(pair, lambda: (a_pair(spot, 1 - low).wait_recv(), a_on(spot, 1 - low))[0])
    if early:
        b_half(half).wait_recv()
        b_spread(1)

    @pl.loop(1, line)
    def _(j):
        z = lax.rem(spot + line - j, line)

        def go():
            a_line(z, spot).wait_recv()
            a_half(ev, z, low).start()
            a_pair(z, low).start()
            a_twin(0, ev, z, low).start()

        when_owner(device(z, low), go)

        def go_pair():
            a_pair(z, 1 - low).wait_recv()
            a_on(z, 1 - low)

        when_owner(device(z, 1 - low), go_pair)

    if early:
        for side in range(2):
            event = (ev, half)[side]
            b_pair(side, spot, 1 - low).wait_recv()
            b_twin(side, event, spot, 1 - low).start()

        @pl.loop(1, line)
        def _(j):
            z = lax.rem(spot + line - j, line)
            for side in range(2):
                event = (ev, half)[side]
                b_line(side, z, spot).wait_recv()
                b_pair(side, z, low).start()
                b_twin(side, event, z, low).start()
            for side in range(2):
                event = (ev, half)[side]
                b_pair(side, z, 1 - low).wait_recv()
                b_twin(side, event, z, 1 - low).start()

    @pl.loop(0, line)
    def _(j):
        z = lax.rem(spot + line - j, line)
        for parity in (low, 1 - low):

            def go():
                a_half(half, z, parity).wait_recv()
                a_twin(1, half, z, parity).start()

            when_owner(device(z, parity), go)

    for index in range(2 * STEPS):
        for k in range(LINKS):
            message(index, k, 1).wait_send()
    for i in range(n_event - 1):
        rate_copy(i).wait_send()

    @pl.loop(0, line)
    def _(z):
        when_owner(device(z, 1 - low), lambda: pair_sum(z, 1 - low).wait_send())
        when_owner(device(z, low), lambda: a_pair(z, low).wait_send())

        @pl.when(z != spot)
        def _():
            when_owner(device(z, low), lambda: line_sum(z, spot).wait_send())
            when_owner(me, lambda: a_line(spot, z).wait_send())

        if early:
            for side in range(2):
                b_pair(side, z, low).wait_send()

                @pl.when(z != spot)
                def _():
                    b_line(side, spot, z).wait_send()

        for parity in range(2):

            def go():
                a_half(ev, z, parity).wait_send()
                a_twin(0, twin, z, parity).wait_recv()
                a_twin(1, twin_half, z, parity).wait_recv()
                a_twin(0, ev, z, parity).wait_send()
                a_twin(1, half, z, parity).wait_send()
                if early:
                    for side in range(2):
                        b_twin(side, (twin, twin_half)[side], z, parity).wait_recv()
                        b_twin(side, (ev, half)[side], z, parity).wait_send()

            when_owner(device(z, parity), go)

    if early:
        b_half(ev).wait_send()


def body(
    n,
    n_event,
    reach_attrs,
    w_first,
    b_first,
    w_second,
    b_second,
    w_out,
    section_factor,
    bed_slope,
    seg_count,
    section_class,
    down_local,
    send_list,
    recv_list,
    area_start,
    lateral,
    cotangent,
):
    f32, bf16 = jnp.float32, jnp.bfloat16
    events, reaches = area_start.shape
    feat, hid = w_first.shape
    class_total = section_factor.shape[0]
    part = hid // n_event
    owners = n if part % (8 * n) == 0 else part // 8
    chunk = part // owners
    scale = 32.0 / math.sqrt(events * n_event * reaches * n)
    one_hot = (section_class[None, :] == jnp.arange(class_total, dtype=jnp.int32)[:, None]).astype(f32)
    k_base = jnp.sqrt(bed_slope) * jnp.sum(one_hot * section_factor[:, None], axis=0)
    position = jnp.arange(reaches, dtype=jnp.int32)
    hop = jnp.where(down_local < reaches, down_local - position, 0).astype(f32)
    rows = jnp.stack([k_base, 1.0 / seg_count.astype(f32), hop], axis=0)
    cols = jnp.stack([b_first, b_second, w_out.astype(f32)], axis=1)
    attrs = jnp.concatenate(
        [reach_attrs.T, jnp.ones((1, reaches), bf16), jnp.zeros((127 - feat, reaches), bf16)], axis=0
    )
    vmem = pl.BlockSpec(memory_space=pltpu.VMEM)
    dma = pltpu.SemaphoreType.DMA
    wide = hid + 128
    outflow, grad_lateral, full = pl.pallas_call(
        functools.partial(kernel, n, n_event, owners, chunk, scale),
        out_shape=(
            jax.ShapeDtypeStruct((events, reaches), f32),
            jax.ShapeDtypeStruct((STEPS, events, reaches), f32),
            jax.ShapeDtypeStruct((hid, wide), f32),
        ),
        in_specs=[vmem] * 11,
        out_specs=(vmem,) * 3,
        scratch_shapes=[
            pltpu.VMEM((hid, reaches), f32),
            pltpu.VMEM((hid, reaches), bf16),
            pltpu.VMEM((hid, reaches), f32),
            pltpu.VMEM((hid, reaches), bf16),
            pltpu.VMEM((hid, reaches), bf16),
            pltpu.VMEM((1, reaches), f32),
            pltpu.VMEM((LINKS * GROUP, reaches), bf16),
            pltpu.VMEM((LINKS * GROUP, reaches), bf16),
            pltpu.VMEM((2 * STEPS, LINKS, 8, 128), f32),
            pltpu.VMEM((2 * STEPS, LINKS, 8, 128), f32),
            pltpu.VMEM((1, reaches), f32),
            pltpu.VMEM((n_event - 1, 1, reaches), f32),
            pltpu.VMEM((part, wide), f32),
            pltpu.VMEM((n // 2, chunk, wide), f32),
            pltpu.VMEM((n // 2, chunk, wide), f32),
            dma((2 * STEPS, LINKS)),
            dma((2 * STEPS, LINKS)),
            dma((n_event - 1,)),
            dma((n_event - 1,)),
            dma((n // 2,)),
            dma((n // 2,)),
            dma((n // 2,)),
            dma((n // 2,)),
            dma((n // 2,)),
            dma((n // 2,)),
            dma((n // 2,)),
            dma((n // 2,)),
            dma((n,)),
            dma((n,)),
            dma((2, n)),
            dma((2, n)),
            dma((2, n // 2)),
            dma((2, n // 2)),
            dma((2, n // 2)),
            dma((2, n // 2)),
            dma,
            dma,
            dma((2, n)),
            dma((2, n)),
        ],
        compiler_params=pltpu.CompilerParams(
            collective_id=0, has_side_effects=True, vmem_limit_bytes=48 * 1024 * 1024
        ),
    )(
        w_first.T, w_second, w_second.T, cols, attrs, rows, send_list, recv_list,
        area_start, lateral, cotangent,
    )
    small = full[:, hid : hid + feat + 3].T
    return (
        outflow,
        grad_lateral,
        small[:feat],
        small[feat],
        full[:, :hid],
        small[feat + 1],
        small[feat + 2],
    )


def solution(mesh):
    return jax.shard_map(
        functools.partial(body, mesh.shape["basin"], mesh.shape["event"]),
        mesh=mesh,
        in_specs=(
            P("basin", None),
            P(),
            P(),
            P(),
            P(),
            P(),
            P(),
            P("basin"),
            P("basin"),
            P("basin"),
            P("basin"),
            P("basin", None, None),
            P("basin", None, None),
            P("event", "basin"),
            P(None, "event", "basin"),
            P("event", "basin"),
        ),
        out_specs=(P("event", "basin"), P(None, "event", "basin"), P(), P(), P(), P(), P()),
        check_vma=False,
    )
```
